128 devices in a mesh: sub: 32 (over x, y, core), grp: 4 (over z).
Axes of the slice: x: 4, y: 4, z: 4, core: 2. Of those that a mesh axis runs over, the one named last changes fastest.
Arguments:
- resid: bfloat16 [1024, 384, 256], P(('sub', 'grp')), may hold values from -6 to 6
- local_inv: bfloat16 [1024, 256, 256], P(('sub', 'grp')), may hold values from -0.375 to 0.375
- basis: bfloat16 [1024, 256, 128], P(('sub', 'grp')), may hold values from -0.375 to 0.375
- coarse_inv: bfloat16 [32768, 256], P(('sub', 'grp')), may hold values from -0.375 to 0.375
- coarse_map: int32 [1024, 128], P(('sub', 'grp')), may hold values from 0 to 32767, as said below
- row_counts: int32 [1024], P(('sub', 'grp')), may hold values from 64 to 128
Outputs:
- correction: float32 [1024, 384, 256], P(('sub', 'grp'))
The draws below stay inside these ranges and needn't reach their ends.
Inputs may be any that keep to these rules, and one draw needn't show every extreme that they name: `coarse_map`: coarse degree of freedom c belongs to owner c // 256. The slots of one device's 8 subdomains name coarse degrees of freedom of any one owner at most 16 times, and every device reaches 16 for some owner.
All inputs are finite; a program needn't handle non-finite values.
Results may differ from the reference program's by a relative error of at most 0.012.
Values may be sent and summed in bfloat16 or wider, within the bound.
No kernel may reach another device: no remote copies, remote signals or barrier semaphores. Data moves between devices by JAX's collectives and lax.ppermute only.
A program may use at most 128 MiB of HBM per device.

```python
import jax
import jax.numpy as jnp
from jax import lax

M = 256
KC = 128
CB = 256
SUBS = 8
R = 384
OWNERS = 128
SUBS_ALL = 1024
NCOARSE = 32768
AVG = 8


def draw_coarse_map(key, part):
    key = jax.random.fold_in(key, 7)
    half = OWNERS // 2
    slots = SUBS * KC

    def one_device(device):
        sub_key = jax.random.fold_in(key, device)
        key_shift, key_order, key_pair, key_local = jax.random.split(sub_key, 4)
        shift = jax.random.randint(key_shift, (half,), 0, AVG + 1)
        shift = shift.at[device % half].set(AVG)
        loads = jnp.concatenate([AVG + shift, AVG - shift])
        paired = jax.random.permutation(key_pair, OWNERS)
        loads = jnp.zeros((OWNERS,), jnp.int32).at[paired].set(loads.astype(jnp.int32))
        owner = jnp.repeat(jnp.arange(OWNERS, dtype=jnp.int32), loads, total_repeat_length=slots)
        owner = jax.random.permutation(key_order, owner)
        local = jax.random.randint(key_local, (slots,), 0, CB)
        return (owner * CB + local).reshape(SUBS, KC)
    maps = jax.vmap(one_device)(jnp.arange(OWNERS, dtype=jnp.int32))
    return maps.reshape(SUBS_ALL, KC).astype(jnp.int32)


def touch_ends(values, rng, smallest, high):
    dims = values.shape
    index_at = [jax.random.randint(jax.random.fold_in(rng, axis), (), 0, dims[axis]) for axis in range(len(dims))]
    values = values.at[tuple(index_at)].set(smallest)
    longest = dims.index(max(dims))
    index_at[longest] = (index_at[longest] + 1) % dims[longest]
    return values.at[tuple(index_at)].set(high)


def block_levels(key, shape, pieces, low, top_value):
    loudness, own = 1.0, jax.random.fold_in(key, 6)
    for position, shards_of in pieces:
        steps = jnp.exp(jax.random.uniform(jax.random.fold_in(own, position), (shards_of,), jnp.float32, low / len(pieces), top_value / len(pieces)))
        loudness = loudness * jnp.repeat(steps, shape[position] // shards_of).reshape([-1 if axis == position else 1 for axis in range(len(shape))])
    return loudness


def noise(own_key, dims, scale, most, shards=(), kind=jnp.bfloat16):
    array = scale * jax.random.normal(own_key, dims, jnp.float32)
    if shards:
        array = array * block_levels(own_key, dims, shards, -0.22, 0.18)
    return jnp.clip(array, -most, most).astype(kind)


def setup_inputs(seed: int = 0) -> dict:
    splits = jax.random.split(jax.random.key(seed), 7)
    resid = noise(splits[0], (SUBS_ALL, R, M), 1.0, 6.0, ((0, 128),))
    local_inv = noise(splits[1], (SUBS_ALL, M, M), M ** -0.5, 0.375, ((0, 128),))
    basis = noise(splits[2], (SUBS_ALL, M, KC), M ** -0.5, 0.375, ((0, 128),))
    coarse_inv = noise(splits[3], (NCOARSE, CB), CB ** -0.5, 0.375, ((0, 128),))
    coarse_map = draw_coarse_map(jax.random.fold_in(splits[6], 71), 0)
    row_counts = touch_ends(jax.random.randint(splits[5], (SUBS_ALL,), KC // 2, KC + 1), jax.random.fold_in(splits[5], 1), KC // 2, KC).astype(jnp.int32)
    return {"resid": resid, "local_inv": local_inv, "basis": basis, "coarse_inv": coarse_inv, "coarse_map": coarse_map, "row_counts": row_counts}


def reference(resid, local_inv, basis, coarse_inv, coarse_map, row_counts):
    live = (jnp.arange(KC, dtype=jnp.int32)[None, :] < row_counts[:, None]).astype(jnp.float32)

    def restrict_block(args):
        base, cols, mask = args
        return jnp.einsum('smk,srm->skr', base.astype(jnp.float32), cols.astype(jnp.float32)) * mask[:, :, None]

    restricted = lax.map(restrict_block, (basis.reshape(OWNERS, SUBS, M, KC), resid.reshape(OWNERS, SUBS, R, M), live.reshape(OWNERS, SUBS, KC)))
    coarse_res = jax.ops.segment_sum(restricted.reshape(SUBS_ALL * KC, R), coarse_map.reshape(-1).astype(jnp.int32), num_segments=NCOARSE)
    coarse_in = coarse_res.astype(jnp.bfloat16).reshape(OWNERS, CB, R)
    coarse_sol = jnp.einsum('oij,ojr->oir', coarse_inv.reshape(OWNERS, CB, CB).astype(jnp.float32), coarse_in.astype(jnp.float32))
    coarse_sol = coarse_sol.astype(jnp.bfloat16).reshape(NCOARSE, R)
    pulled = coarse_sol[coarse_map.astype(jnp.int32)] * live[:, :, None].astype(jnp.bfloat16)

    def apply_block(args):
        inverse, cols, base, back = args
        local = jnp.einsum('smn,srn->srm', inverse.astype(jnp.float32), cols.astype(jnp.float32))
        return local + jnp.einsum('smk,skr->srm', base.astype(jnp.float32), back.astype(jnp.float32))

    out = lax.map(apply_block, (local_inv.reshape(OWNERS, SUBS, M, M), resid.reshape(OWNERS, SUBS, R, M), basis.reshape(OWNERS, SUBS, M, KC), pulled.reshape(OWNERS, SUBS, KC, R)))
    return out.reshape(SUBS_ALL, R, M)
```

```python
import functools

import jax
import jax.numpy as jnp
from jax import lax
from jax.experimental import pallas as pl
from jax.experimental.pallas import tpu as pltpu
from jax.sharding import PartitionSpec as P

CAP = 16
LANES = 128
IDROWS = 8
F32 = jnp.float32
BF16 = jnp.bfloat16
AXES = ("sub", "grp")
NT = (((1,), (1,)), ((), ()))
TN = (((0,), (0,)), ((), ()))


def iota(shape, axis):
    return lax.broadcasted_iota(jnp.int32, shape, axis)


def dot(a, b, dims=(((1,), (0,)), ((), ()))):
    return lax.dot_general(a, b, dims, preferred_element_type=F32)


def pack_kernel(
    me_ref, counts_ref, map_ref, resid_hbm, basis_hbm, send_hbm, slot_ref,
    resid_v, basis_v, rest_v, send_v, in_sem, out_sem,
):
    subs, rcols, _ = resid_hbm.shape
    slots_per = basis_hbm.shape[2]
    owners = send_hbm.shape[0]
    blocks = rcols // LANES
    loads = []
    for s in range(subs):
        pair = (
            pltpu.make_async_copy(basis_hbm.at[s], basis_v.at[s], in_sem.at[0, s]),
            pltpu.make_async_copy(resid_hbm.at[s], resid_v.at[s], in_sem.at[1, s]),
        )
        for copy in pair:
            copy.start()
        loads.append(pair)

    lane = iota((1, slots_per), 1)
    row = iota((owners, slots_per), 0)
    before = jnp.where(
        iota((slots_per, 2 * slots_per), 0) < iota((slots_per, 2 * slots_per), 1), 1.0, 0.0
    ).astype(BF16)
    group = lax.rem(me_ref[0], LANES // CAP)
    id_place = jnp.where(row // CAP == group, lax.rem(row, CAP), -1)
    taken = jnp.zeros((owners, slots_per), F32)
    table = jnp.zeros((owners, LANES), F32)
    slot_rows = []
    for s in range(subs):
        ids = map_ref[s : s + 1, :]
        live = lane < counts_ref[s]
        target = jnp.where(live, ids // 256, -1)
        within = lax.rem(ids, 256) + 1
        hit = row == target
        onehot = jnp.where(hit, 1.0, 0.0).astype(BF16)
        sums = dot(onehot, before)
        rank = jnp.sum(jnp.where(hit, sums[:, :slots_per] + taken, 0.0), axis=0, keepdims=True)
        taken = taken + sums[:, slots_per:]
        rank = rank.astype(jnp.int32)
        named = jnp.where(id_place == rank, within, 0).astype(F32).astype(BF16)
        table = table + dot(onehot, named, NT)
        slot = jnp.where(live, target * CAP + rank, -1)
        slot_ref[s : s + 1, :] = slot
        slot_rows.append(slot)
    send_v[:, blocks * CAP :, :] = jnp.broadcast_to(
        table[:, None, :], (owners, IDROWS, LANES)
    ).astype(BF16)

    for s in range(subs):
        for copy in loads[s]:
            copy.wait()
        rest_v[:, s * slots_per : (s + 1) * slots_per] = dot(resid_v[s], basis_v[s]).astype(BF16)

    tile = LANES // CAP * 2
    slots = jnp.concatenate(slot_rows, axis=1)
    place = iota((tile * CAP, slots.shape[1]), 0)
    stores = []
    for t in range(owners // tile):
        pick = jnp.where(place == slots - t * tile * CAP, 1.0, 0.0).astype(BF16)
        part = dot(pick, rest_v[...], NT).astype(BF16).reshape(tile, CAP, rcols)
        for q in range(blocks):
            send_v[t * tile : (t + 1) * tile, q * CAP : (q + 1) * CAP, :] = part[
                :, :, q * LANES : (q + 1) * LANES
            ]
        copy = pltpu.make_async_copy(
            send_v.at[pl.ds(t * tile, tile)], send_hbm.at[pl.ds(t * tile, tile)], out_sem.at[t]
        )
        copy.start()
        stores.append(copy)
    for copy in stores:
        copy.wait()


def owner_kernel(recv_hbm, inv_ref, back_hbm, recv_v, back_v, match_v, in_sem, out_sem):
    owners = recv_hbm.shape[0]
    rcols = back_hbm.shape[2]
    blocks = rcols // LANES
    cblock = inv_ref.shape[0]
    tile = LANES // CAP * 2
    rows = tile * CAP
    tiles = owners // tile
    loads = []
    for t in range(tiles):
        copy = pltpu.make_async_copy(
            recv_hbm.at[pl.ds(t * tile, tile)], recv_v.at[pl.ds(t * tile, tile)], in_sem.at[t]
        )
        copy.start()
        loads.append(copy)
    dof = iota((cblock, LANES), 0) + 1
    total = jnp.zeros((cblock, rcols), F32)
    for t in range(tiles):
        loads[t].wait()
        halves = []
        for h in range(2):
            start = t * tile + h * (tile // 2)
            named = recv_v[start : start + tile // 2, blocks * CAP :, :].astype(F32)
            named = jnp.sum(named, axis=0)[0:1, :].astype(jnp.int32)
            halves.append(jnp.where(dof == named, 1.0, 0.0).astype(BF16))
        match = jnp.concatenate(halves, axis=1)
        match_v[:, t * rows : (t + 1) * rows] = match
        got = jnp.concatenate(
            [
                recv_v[t * tile : (t + 1) * tile, q * CAP : (q + 1) * CAP, :].reshape(rows, LANES)
                for q in range(blocks)
            ],
            axis=1,
        )
        total = total + dot(match, got)
    sol = dot(inv_ref[...], total.astype(BF16)).astype(BF16)
    stores = []
    for t in range(tiles):
        part = dot(match_v[:, t * rows : (t + 1) * rows], sol, TN).astype(BF16)
        back_v[t * tile : (t + 1) * tile] = part.reshape(tile, CAP, rcols)
        copy = pltpu.make_async_copy(
            back_v.at[pl.ds(t * tile, tile)], back_hbm.at[pl.ds(t * tile, tile)], out_sem.at[t]
        )
        copy.start()
        stores.append(copy)
    for copy in stores:
        copy.wait()


def finish_kernel(
    back_hbm, slot_ref, resid_hbm, inv_hbm, basis_hbm, out_hbm,
    back_v, resid_v, inv_v, basis_v, pulled_v, out_v, back_sem, in_sem, out_sem,
):
    subs, rcols, _ = resid_hbm.shape
    slots_per = basis_hbm.shape[2]
    owners = back_hbm.shape[0]
    whole = pltpu.make_async_copy(back_hbm, back_v, back_sem)
    whole.start()
    loads = []
    for s in range(subs):
        group = (
            pltpu.make_async_copy(resid_hbm.at[s], resid_v.at[s], in_sem.at[0, s]),
            pltpu.make_async_copy(inv_hbm.at[s], inv_v.at[s], in_sem.at[1, s]),
            pltpu.make_async_copy(basis_hbm.at[s], basis_v.at[s], in_sem.at[2, s]),
        )
        for copy in group:
            copy.start()
        loads.append(group)
    whole.wait()
    back = back_v[...].reshape(owners * CAP, rcols)
    place = iota((owners * CAP, 2 * slots_per), 0)
    for s in range(0, subs, 2):
        slots = jnp.concatenate([slot_ref[s : s + 1, :], slot_ref[s + 1 : s + 2, :]], axis=1)
        pick = jnp.where(place == slots, 1.0, 0.0).astype(BF16)
        pulled_v[:, s * slots_per : (s + 2) * slots_per] = dot(back, pick, TN).astype(BF16)
    stores = []
    for s in range(subs):
        for copy in loads[s]:
            copy.wait()
        out_v[s] = dot(resid_v[s], inv_v[s], NT) + dot(
            pulled_v[:, s * slots_per : (s + 1) * slots_per], basis_v[s], NT
        )
        copy = pltpu.make_async_copy(out_v.at[s], out_hbm.at[s], out_sem.at[s])
        copy.start()
        stores.append(copy)
    for copy in stores:
        copy.wait()


ANY = pl.BlockSpec(memory_space=pl.ANY)
INVMEM = pl.BlockSpec(memory_space=pltpu.VMEM)
INSMEM = pl.BlockSpec(memory_space=pltpu.SMEM)


def per_device(resid, local_inv, basis, coarse_inv, coarse_map, row_counts):
    subs, rcols, width = resid.shape
    slots_per = basis.shape[2]
    slots = subs * slots_per
    owners = lax.axis_size("sub") * lax.axis_size("grp")
    blocks = rcols // LANES
    tiles = owners // (2 * LANES // CAP)
    sem = pltpu.SemaphoreType.DMA
    params = pltpu.CompilerParams(vmem_limit_bytes=40 * 1024 * 1024)
    me = lax.axis_index(AXES).astype(jnp.int32).reshape(1)
    packed = (owners, blocks * CAP + IDROWS, LANES)
    send, slot = pl.pallas_call(
        pack_kernel,
        out_shape=(
            jax.ShapeDtypeStruct(packed, BF16),
            jax.ShapeDtypeStruct((subs, slots_per), jnp.int32),
        ),
        in_specs=[INSMEM, INSMEM, INVMEM, ANY, ANY],
        out_specs=(ANY, INVMEM),
        scratch_shapes=[
            pltpu.VMEM(resid.shape, BF16),
            pltpu.VMEM(basis.shape, BF16),
            pltpu.VMEM((rcols, slots), BF16),
            pltpu.VMEM(packed, BF16),
            sem((2, subs)),
            sem((tiles,)),
        ],
        compiler_params=params,
        name="pack",
    )(me, row_counts, coarse_map, resid, basis)
    recv = lax.all_to_all(send, AXES, split_axis=0, concat_axis=0, tiled=True)
    chunk = (owners, CAP, rcols)
    back = pl.pallas_call(
        owner_kernel,
        out_shape=jax.ShapeDtypeStruct(chunk, BF16),
        in_specs=[ANY, INVMEM],
        out_specs=ANY,
        scratch_shapes=[
            pltpu.VMEM(packed, BF16),
            pltpu.VMEM(chunk, BF16),
            pltpu.VMEM((coarse_inv.shape[0], owners * CAP), BF16),
            sem((tiles,)),
            sem((tiles,)),
        ],
        compiler_params=params,
        name="owner",
    )(recv, coarse_inv)
    back = lax.all_to_all(back, AXES, split_axis=0, concat_axis=0, tiled=True)
    return pl.pallas_call(
        finish_kernel,
        out_shape=jax.ShapeDtypeStruct((subs, rcols, width), F32),
        in_specs=[ANY, INVMEM, ANY, ANY, ANY],
        out_specs=ANY,
        scratch_shapes=[
            pltpu.VMEM(chunk, BF16),
            pltpu.VMEM(resid.shape, BF16),
            pltpu.VMEM(local_inv.shape, BF16),
            pltpu.VMEM(basis.shape, BF16),
            pltpu.VMEM((rcols, slots), BF16),
            pltpu.VMEM((subs, rcols, width), F32),
            sem,
            sem((3, subs)),
            sem((subs,)),
        ],
        compiler_params=params,
        name="finish",
    )(back, slot, resid, local_inv, basis)


def solution(mesh):
    placed = (
        P(("sub", "grp"), None, None),
        P(("sub", "grp"), None, None),
        P(("sub", "grp"), None, None),
        P(("sub", "grp"), None),
        P(("sub", "grp"), None),
        P(("sub", "grp")),
    )
    return jax.shard_map(
        per_device,
        mesh=mesh,
        in_specs=placed,
        out_specs=P(("sub", "grp"), None, None),
        check_vma=False,
    )
```

```python
import jax
import jax.numpy as jnp
from jax import lax
from jax.experimental import pallas as pl
from jax.experimental.pallas import tpu as pltpu
from jax.sharding import PartitionSpec as P

CAP = 16
LANES = 128
IDROWS = 8
F32 = jnp.float32
BF16 = jnp.bfloat16
AXES = ("sub", "grp")
NT = (((1,), (1,)), ((), ()))
TN = (((0,), (0,)), ((), ()))


def iota(shape, axis):
    return lax.broadcasted_iota(jnp.int32, shape, axis)


def dot(a, b, dims=(((1,), (0,)), ((), ()))):
    return lax.dot_general(a, b, dims, preferred_element_type=F32)


def pack_kernel(
    me_ref, counts_hbm, map_hbm, resid_hbm, basis_hbm, send_ref, slot_ref,
    counts_v, map_v, resid_v, basis_v, rest_v, small_sem, in_sem,
):
    subs, rcols, _ = resid_hbm.shape
    slots_per = basis_hbm.shape[2]
    owners = send_ref.shape[0]
    blocks = rcols // LANES
    small = (
        pltpu.make_async_copy(map_hbm, map_v, small_sem.at[0]),
        pltpu.make_async_copy(counts_hbm, counts_v, small_sem.at[1]),
    )
    for copy in small:
        copy.start()
    loads = []
    for s in range(subs):
        pair = (
            pltpu.make_async_copy(basis_hbm.at[s], basis_v.at[s], in_sem.at[0, s]),
            pltpu.make_async_copy(resid_hbm.at[s], resid_v.at[s], in_sem.at[1, s]),
        )
        for copy in pair:
            copy.start()
        loads.append(pair)
    for copy in small:
        copy.wait()

    lane = iota((1, slots_per), 1)
    row = iota((owners, slots_per), 0)
    before = jnp.where(
        iota((slots_per, 2 * slots_per), 0) < iota((slots_per, 2 * slots_per), 1), 1.0, 0.0
    ).astype(BF16)
    group = lax.rem(me_ref[0], LANES // CAP)
    id_row = iota((LANES, slots_per), 0)
    id_place = jnp.where(id_row // CAP == group, lax.rem(id_row, CAP), -1)
    targets = [
        jnp.where(lane < counts_v[s], map_v[s : s + 1, :] // 256, -1) for s in range(subs)
    ]
    hits = [row == target for target in targets]
    onehot = jnp.concatenate([jnp.where(hit, 1.0, 0.0).astype(BF16) for hit in hits], axis=0)
    sums = dot(onehot, before)
    taken = jnp.zeros((owners, slots_per), F32)
    slot_rows = []
    for s in range(subs):
        own = sums[s * owners : (s + 1) * owners]
        rank = jnp.sum(jnp.where(hits[s], own[:, :slots_per] + taken, 0.0), axis=0, keepdims=True)
        taken = taken + own[:, slots_per:]
        rank = rank.astype(jnp.int32)
        within = lax.rem(map_v[s : s + 1, :], 256) + 1
        slot = jnp.where(targets[s] < 0, -1, targets[s] * CAP + rank)
        rest_v[rcols:, s * slots_per : (s + 1) * slots_per] = (
            jnp.where(id_place == rank, within, 0).astype(F32).astype(BF16)
        )
        slot_ref[s : s + 1, :] = slot
        slot_rows.append(slot)

    for s in range(subs):
        for copy in loads[s]:
            copy.wait()
        rest_v[:rcols, s * slots_per : (s + 1) * slots_per] = dot(
            resid_v[s], basis_v[s]
        ).astype(BF16)

    tile = LANES // CAP * 2
    slots = jnp.concatenate(slot_rows, axis=1)
    place = iota((tile * CAP, slots.shape[1]), 0)
    for t in range(owners // tile):
        pick = jnp.where(place == slots - t * tile * CAP, 1.0, 0.0).astype(BF16)
        part = dot(pick, rest_v[...], NT)
        mine = slice(t * tile, (t + 1) * tile)
        for q in range(blocks):
            send_ref[mine, q * CAP : (q + 1) * CAP, :] = (
                part[:, q * LANES : (q + 1) * LANES].astype(BF16).reshape(tile, CAP, LANES)
            )
        named = part[:, rcols:].reshape(tile, CAP // IDROWS, IDROWS, LANES)
        send_ref[mine, blocks * CAP :, :] = jnp.sum(named, axis=1).astype(BF16)


def owner_kernel(recv_ref, inv_ref, back_ref, got_v, match_v):
    owners, _, rcols = back_ref.shape
    blocks = rcols // LANES
    cblock = inv_ref.shape[0]
    step = LANES // CAP
    dof = iota((cblock, LANES), 0) + 1
    for t in range(owners // step):
        mine = slice(t * step, (t + 1) * step)
        rows = slice(t * LANES, (t + 1) * LANES)
        named = jnp.sum(recv_ref[mine, blocks * CAP :, :].astype(F32), axis=0)
        named = jnp.sum(named, axis=0, keepdims=True).astype(jnp.int32)
        match_v[:, rows] = jnp.where(dof == named, 1.0, 0.0).astype(BF16)
        for q in range(blocks):
            got_v[rows, q * LANES : (q + 1) * LANES] = recv_ref[
                mine, q * CAP : (q + 1) * CAP, :
            ].reshape(LANES, LANES)
    total = dot(match_v[...], got_v[...])
    sol = dot(inv_ref[...], total.astype(BF16)).astype(BF16)
    tile = 4 * step
    for t in range(owners // tile):
        part = dot(match_v[:, t * tile * CAP : (t + 1) * tile * CAP], sol, TN).astype(BF16)
        back_ref[t * tile : (t + 1) * tile] = part.reshape(tile, CAP, rcols)


def local_kernel(resid_ref, inv_ref, out_ref):
    for s in range(resid_ref.shape[0]):
        out_ref[s] = dot(resid_ref[s], inv_ref[s], NT)


def finish_kernel(back_ref, slot_ref, local_ref, basis_ref, out_hbm, pulled_v, out_v, out_sem):
    subs, rcols, _ = local_ref.shape
    slots_per = basis_ref.shape[2]
    owners = back_ref.shape[0]
    back = back_ref[...].reshape(owners * CAP, rcols)
    place = iota((owners * CAP, subs * slots_per), 0)
    slots = jnp.concatenate([slot_ref[s : s + 1, :] for s in range(subs)], axis=1)
    pick = jnp.where(place == slots, 1.0, 0.0).astype(BF16)
    pulled_v[...] = dot(back, pick, TN).astype(BF16)
    stores = []
    for s in range(subs):
        out_v[s] = local_ref[s] + dot(
            pulled_v[:, s * slots_per : (s + 1) * slots_per], basis_ref[s], NT
        )
        copy = pltpu.make_async_copy(out_v.at[s], out_hbm.at[s], out_sem.at[s])
        copy.start()
        stores.append(copy)
    for copy in stores:
        copy.wait()


ANY = pl.BlockSpec(memory_space=pl.ANY)
HBM = pl.BlockSpec(memory_space=pltpu.HBM)
INVMEM = pl.BlockSpec(memory_space=pltpu.VMEM)
INSMEM = pl.BlockSpec(memory_space=pltpu.SMEM)


def params(mib):
    return pltpu.CompilerParams(vmem_limit_bytes=mib * 1024 * 1024)


def pack(me, counts, cmap, resid, basis, owners):
    subs, rcols, _ = resid.shape
    slots_per = basis.shape[2]
    shape = (owners, rcols // LANES * CAP + IDROWS, LANES)
    return pl.pallas_call(
        pack_kernel,
        out_shape=(
            jax.ShapeDtypeStruct(shape, BF16),
            jax.ShapeDtypeStruct((subs, slots_per), jnp.int32),
        ),
        in_specs=[INSMEM, HBM, HBM, HBM, HBM],
        out_specs=(INVMEM, INVMEM),
        scratch_shapes=[
            pltpu.SMEM(counts.shape, jnp.int32),
            pltpu.VMEM(cmap.shape, jnp.int32),
            pltpu.VMEM(resid.shape, BF16),
            pltpu.VMEM(basis.shape, BF16),
            pltpu.VMEM((rcols + LANES, subs * slots_per), BF16),
            pltpu.SemaphoreType.DMA((2,)),
            pltpu.SemaphoreType.DMA((2, subs)),
        ],
        compiler_params=params(24),
        name="pack",
    )(me, counts, cmap, resid, basis)


def owner(recv, inv, rcols):
    owners = recv.shape[0]
    return pl.pallas_call(
        owner_kernel,
        out_shape=jax.ShapeDtypeStruct((owners, CAP, rcols), BF16),
        in_specs=[INVMEM, INVMEM],
        out_specs=INVMEM,
        scratch_shapes=[
            pltpu.VMEM((owners * CAP, rcols), BF16),
            pltpu.VMEM((inv.shape[0], owners * CAP), BF16),
        ],
        compiler_params=params(24),
        name="owner",
    )(recv, inv)


def local_solve(resid, inv):
    subs, rcols, width = resid.shape
    return pl.pallas_call(
        local_kernel,
        out_shape=jax.ShapeDtypeStruct(resid.shape, F32),
        in_specs=[INVMEM, INVMEM],
        out_specs=INVMEM,
        compiler_params=params(24),
        cost_estimate=pl.CostEstimate(
            flops=2 * subs * rcols * width * width,
            bytes_accessed=2 * (resid.size + inv.size) + 4 * resid.size,
            transcendentals=0,
        ),
        name="local",
    )(resid, inv)


def finish(back, slot, local, basis):
    subs, rcols, _ = local.shape
    slots_per = basis.shape[2]
    return pl.pallas_call(
        finish_kernel,
        out_shape=jax.ShapeDtypeStruct(local.shape, F32),
        in_specs=[INVMEM, INVMEM, INVMEM, INVMEM],
        out_specs=ANY,
        scratch_shapes=[
            pltpu.VMEM((rcols, subs * slots_per), BF16),
            pltpu.VMEM(local.shape, F32),
            pltpu.SemaphoreType.DMA((subs,)),
        ],
        compiler_params=params(32),
        name="finish",
    )(back, slot, local, basis)


def per_device(resid, local_inv, basis, coarse_inv, coarse_map, row_counts):
    owners = lax.axis_size("sub") * lax.axis_size("grp")
    me = lax.axis_index(AXES).astype(jnp.int32).reshape(1)
    send, slot = pack(me, row_counts, coarse_map, resid, basis, owners)
    recv = lax.all_to_all(send, AXES, split_axis=0, concat_axis=0, tiled=True)
    local = local_solve(resid, local_inv)
    back = owner(recv, coarse_inv, resid.shape[1])
    back = lax.all_to_all(back, AXES, split_axis=0, concat_axis=0, tiled=True)
    return finish(back, slot, local, basis)


def solution(mesh):
    placed = (
        P(("sub", "grp"), None, None),
        P(("sub", "grp"), None, None),
        P(("sub", "grp"), None, None),
        P(("sub", "grp"), None),
        P(("sub", "grp"), None),
        P(("sub", "grp")),
    )
    return jax.shard_map(
        per_device,
        mesh=mesh,
        in_specs=placed,
        out_specs=P(("sub", "grp"), None, None),
        check_vma=False,
    )
```

```python
import jax
import jax.numpy as jnp
from jax import lax
from jax.experimental import pallas as pl
from jax.experimental.pallas import tpu as pltpu
from jax.sharding import PartitionSpec as P

CAP = 16
LANES = 128
IDROWS = 8
PACK_TILE = 16
OWNER_WIDE = 16
FINISH_BATCH = 8
F32 = jnp.float32
BF16 = jnp.bfloat16
AXES = ("sub", "grp")
NT = (((1,), (1,)), ((), ()))
TN = (((0,), (0,)), ((), ()))


def iota(shape, axis):
    return lax.broadcasted_iota(jnp.int32, shape, axis)


def dot(a, b, dims=(((1,), (0,)), ((), ()))):
    return lax.dot_general(a, b, dims, preferred_element_type=F32)


def pack_kernel(
    me_ref, counts_hbm, map_hbm, resid_hbm, basis_hbm, send_ref, slot_ref,
    counts_v, map_v, resid_v, basis_v, rest_v, row_v, small_sem, in_sem,
):
    subs, rcols, _ = resid_hbm.shape
    slots_per = basis_hbm.shape[2]
    owners = send_ref.shape[0]
    blocks = rcols // LANES
    small = (
        pltpu.make_async_copy(map_hbm, map_v, small_sem.at[0]),
        pltpu.make_async_copy(counts_hbm, counts_v, small_sem.at[1]),
    )
    for copy in small:
        copy.start()

    def loads(s):
        return (
            pltpu.make_async_copy(basis_hbm.at[s], basis_v.at[s], in_sem.at[0, s]),
            pltpu.make_async_copy(resid_hbm.at[s], resid_v.at[s], in_sem.at[1, s]),
        )

    for s in range(subs):
        for copy in loads(s):
            copy.start()
    for copy in small:
        copy.wait()

    lane = iota((1, slots_per), 1)
    row = iota((owners, slots_per), 0)
    before = jnp.where(
        iota((slots_per, 2 * slots_per), 0) < iota((slots_per, 2 * slots_per), 1), 1.0, 0.0
    ).astype(BF16)
    group = lax.rem(me_ref[0], LANES // CAP)
    id_row = iota((LANES, slots_per), 0)
    id_place = jnp.where(id_row // CAP == group, lax.rem(id_row, CAP), -1)
    targets = [
        jnp.where(lane < counts_v[s], map_v[s : s + 1, :] // 256, -1) for s in range(subs)
    ]
    hits = [row == target for target in targets]
    onehot = jnp.concatenate([jnp.where(hit, 1.0, 0.0).astype(BF16) for hit in hits], axis=0)
    sums = dot(onehot, before)
    taken = jnp.zeros((owners, slots_per), F32)
    for s in range(subs):
        own = sums[s * owners : (s + 1) * owners]
        rank = jnp.sum(jnp.where(hits[s], own[:, :slots_per] + taken, 0.0), axis=0, keepdims=True)
        taken = taken + own[:, slots_per:]
        rank = rank.astype(jnp.int32)
        within = lax.rem(map_v[s : s + 1, :], 256) + 1
        slot = jnp.where(targets[s] < 0, -1, targets[s] * CAP + rank)
        rest_v[rcols:, s * slots_per : (s + 1) * slots_per] = (
            jnp.where(id_place == rank, within, 0).astype(F32).astype(BF16)
        )
        slot_ref[s : s + 1, :] = slot
        row_v[:, s * slots_per : (s + 1) * slots_per] = jnp.broadcast_to(slot, (8, slots_per))

    @pl.loop(0, subs)
    def _(s):
        for copy in loads(s):
            copy.wait()
        columns = pl.ds(pl.multiple_of(s * slots_per, slots_per), slots_per)
        rest_v[:rcols, columns] = dot(resid_v[s], basis_v[s]).astype(BF16)

    tile = LANES // CAP * PACK_TILE

    @pl.loop(0, owners // tile)
    def _(t):
        place = iota((tile * CAP, subs * slots_per), 0)
        pick = jnp.where(place == row_v[0:1, :] - t * (tile * CAP), 1.0, 0.0).astype(BF16)
        part = dot(pick, rest_v[...], NT)
        mine = pl.ds(t * tile, tile)
        for q in range(blocks):
            send_ref[mine, q * CAP : (q + 1) * CAP, :] = (
                part[:, q * LANES : (q + 1) * LANES].astype(BF16).reshape(tile, CAP, LANES)
            )
        named = part[:, rcols:].reshape(tile, CAP // IDROWS, IDROWS, LANES)
        send_ref[mine, blocks * CAP :, :] = jnp.sum(named, axis=1).astype(BF16)


def owner_kernel(recv_ref, inv_ref, back_ref, got_v, match_v, total_v):
    owners, _, rcols = back_ref.shape
    blocks = rcols // LANES
    cblock = inv_ref.shape[0]
    step = LANES // CAP
    wide = OWNER_WIDE
    total_v[...] = jnp.zeros_like(total_v)

    @pl.loop(0, owners // (wide * step))
    def _(t):
        dof = iota((cblock, LANES), 0) + 1
        for u in range(wide):
            mine = pl.ds((t * wide + u) * step, step)
            rows = slice(u * LANES, (u + 1) * LANES)
            named = jnp.sum(recv_ref[mine, blocks * CAP :, :].astype(F32), axis=0)
            named = jnp.sum(named, axis=0, keepdims=True).astype(jnp.int32)
            match_v[t, :, rows] = jnp.where(dof == named, 1.0, 0.0).astype(BF16)
            for q in range(blocks):
                got_v[rows, q * LANES : (q + 1) * LANES] = recv_ref[
                    mine, q * CAP : (q + 1) * CAP, :
                ].reshape(LANES, LANES)
        total_v[...] += dot(match_v[t], got_v[...])

    sol = dot(inv_ref[...], total_v[...].astype(BF16)).astype(BF16)

    @pl.loop(0, owners // (wide * step))
    def _(t):
        part = dot(match_v[t], sol, TN).astype(BF16)
        back_ref[pl.ds(t * wide * step, wide * step)] = part.reshape(wide * step, CAP, rcols)


def finish_kernel(
    back_ref, slot_ref, resid_ref, inv_ref, basis_ref, out_hbm, turned_v, row_v, out_v, out_sem
):
    subs, rcols, _ = resid_ref.shape
    slots_per = basis_ref.shape[2]
    rows = back_ref.shape[0] * CAP
    turned_v[...] = back_ref[...].reshape(rows, rcols).T
    batch = FINISH_BATCH
    for s in range(subs):
        row_v[s // batch, :, s % batch * slots_per : (s % batch + 1) * slots_per] = (
            jnp.broadcast_to(slot_ref[s : s + 1, :], (8, slots_per))
        )

    def store(s):
        return pltpu.make_async_copy(out_v.at[s], out_hbm.at[s], out_sem.at[s])

    @pl.loop(0, subs // batch)
    def _(t):
        place = iota((rows, batch * slots_per), 0)
        pick = jnp.where(place == row_v[t, 0:1, :], 1.0, 0.0).astype(BF16)
        pulled = dot(turned_v[...], pick).astype(BF16)
        for i in range(batch):
            s = t * batch + i
            out_v[s] = dot(resid_ref[s], inv_ref[s], NT) + dot(
                pulled[:, i * slots_per : (i + 1) * slots_per], basis_ref[s], NT
            )
            store(s).start()

    for s in range(subs):
        store(s).wait()


ANY = pl.BlockSpec(memory_space=pl.ANY)
HBM = pl.BlockSpec(memory_space=pltpu.HBM)
INVMEM = pl.BlockSpec(memory_space=pltpu.VMEM)
INSMEM = pl.BlockSpec(memory_space=pltpu.SMEM)


def params(mib):
    return pltpu.CompilerParams(vmem_limit_bytes=mib * 1024 * 1024)


def pack(me, counts, cmap, resid, basis, owners):
    subs, rcols, _ = resid.shape
    slots_per = basis.shape[2]
    shape = (owners, rcols // LANES * CAP + IDROWS, LANES)
    return pl.pallas_call(
        pack_kernel,
        out_shape=(
            jax.ShapeDtypeStruct(shape, BF16),
            jax.ShapeDtypeStruct((subs, slots_per), jnp.int32),
        ),
        in_specs=[INSMEM, HBM, HBM, HBM, HBM],
        out_specs=(INVMEM, INVMEM),
        scratch_shapes=[
            pltpu.SMEM(counts.shape, jnp.int32),
            pltpu.VMEM(cmap.shape, jnp.int32),
            pltpu.VMEM(resid.shape, BF16),
            pltpu.VMEM(basis.shape, BF16),
            pltpu.VMEM((rcols + LANES, subs * slots_per), BF16),
            pltpu.VMEM((8, subs * slots_per), jnp.int32),
            pltpu.SemaphoreType.DMA((2,)),
            pltpu.SemaphoreType.DMA((2, subs)),
        ],
        compiler_params=params(24),
        name="pack",
    )(me, *[pltpu.with_memory_space_constraint(x, pltpu.HBM) for x in (counts, cmap, resid, basis)])


def owner(recv, inv, rcols):
    owners = recv.shape[0]
    return pl.pallas_call(
        owner_kernel,
        out_shape=jax.ShapeDtypeStruct((owners, CAP, rcols), BF16),
        in_specs=[INVMEM, INVMEM],
        out_specs=INVMEM,
        scratch_shapes=[
            pltpu.VMEM((OWNER_WIDE * LANES, rcols), BF16),
            pltpu.VMEM(
                (owners * CAP // (OWNER_WIDE * LANES), inv.shape[0], OWNER_WIDE * LANES), BF16
            ),
            pltpu.VMEM((inv.shape[0], rcols), F32),
        ],
        compiler_params=params(24),
        name="owner",
    )(recv, inv)


def finish(back, slot, resid, inv, basis):
    subs, rcols, _ = resid.shape
    rows = back.shape[0] * CAP
    return pl.pallas_call(
        finish_kernel,
        out_shape=jax.ShapeDtypeStruct(resid.shape, F32),
        in_specs=[INVMEM] * 5,
        out_specs=ANY,
        scratch_shapes=[
            pltpu.VMEM((rcols, rows), BF16),
            pltpu.VMEM((subs // FINISH_BATCH, 8, FINISH_BATCH * basis.shape[2]), jnp.int32),
            pltpu.VMEM(resid.shape, F32),
            pltpu.SemaphoreType.DMA((subs,)),
        ],
        compiler_params=params(32),
        name="finish",
    )(back, slot, resid, inv, basis)


def per_device(resid, local_inv, basis, coarse_inv, coarse_map, row_counts):
    owners = lax.axis_size("sub") * lax.axis_size("grp")
    me = lax.axis_index(AXES).astype(jnp.int32).reshape(1)
    send, slot = pack(me, row_counts, coarse_map, resid, basis, owners)
    recv = lax.all_to_all(send, AXES, split_axis=0, concat_axis=0, tiled=True)
    back = owner(recv, coarse_inv, resid.shape[1])
    back = lax.all_to_all(back, AXES, split_axis=0, concat_axis=0, tiled=True)
    return finish(back, slot, resid, local_inv, basis)


def solution(mesh):
    placed = (
        P(("sub", "grp"), None, None),
        P(("sub", "grp"), None, None),
        P(("sub", "grp"), None, None),
        P(("sub", "grp"), None),
        P(("sub", "grp"), None),
        P(("sub", "grp")),
    )
    return jax.shard_map(
        per_device,
        mesh=mesh,
        in_specs=placed,
        out_specs=P(("sub", "grp"), None, None),
        check_vma=False,
    )
```

```python
import jax
import jax.numpy as jnp
from jax import lax
from jax.experimental import pallas as pl
from jax.experimental.pallas import tpu as pltpu
from jax.sharding import PartitionSpec as P

CAP = 16
LANES = 128
IDROWS = 8
OWNER_WIDE = 16
FINISH_BATCH = 8
F32 = jnp.float32
BF16 = jnp.bfloat16
AXES = ("sub", "grp")
NT = (((1,), (1,)), ((), ()))
TN = (((0,), (0,)), ((), ()))


def iota(shape, axis):
    return lax.broadcasted_iota(jnp.int32, shape, axis)


def dot(a, b, dims=(((1,), (0,)), ((), ()))):
    return lax.dot_general(a, b, dims, preferred_element_type=F32)


def pack_kernel(
    me_ref, counts_hbm, map_hbm, resid_hbm, basis_hbm, send_ref, slot_ref,
    counts_v, map_v, resid_v, basis_v, rest_v, comp_v, first_v, first_s, small_sem, in_sem, first_sem,
):
    subs, rcols, _ = resid_hbm.shape
    slots_per = basis_hbm.shape[2]
    slots = subs * slots_per
    owners = send_ref.shape[0]
    blocks = rcols // LANES
    small = (
        pltpu.make_async_copy(map_hbm, map_v, small_sem.at[0]),
        pltpu.make_async_copy(counts_hbm, counts_v, small_sem.at[1]),
    )
    large = (
        pltpu.make_async_copy(basis_hbm, basis_v, in_sem.at[0]),
        pltpu.make_async_copy(resid_hbm, resid_v, in_sem.at[1]),
    )
    for copy in small + large:
        copy.start()
    for copy in small:
        copy.wait()

    lane = iota((1, slots_per), 1)
    row = iota((owners, slots_per), 0)
    before = jnp.where(
        iota((slots_per, 2 * slots_per), 0) < iota((slots_per, 2 * slots_per), 1), 1.0, 0.0
    ).astype(BF16)
    group = lax.rem(me_ref[0], LANES // CAP)
    id_row = iota((LANES, slots_per), 0)
    id_place = jnp.where(id_row // CAP == group, lax.rem(id_row, CAP), -1)
    targets = [
        jnp.where(lane < counts_v[s], map_v[s : s + 1, :] // 256, owners) for s in range(subs)
    ]
    hits = [row == target for target in targets]
    onehots = [jnp.where(hit, 1.0, 0.0).astype(BF16) for hit in hits]
    lower = jnp.concatenate(
        [jnp.where(row > target, 1.0, 0.0).astype(BF16) for target in targets], axis=1
    )
    first = dot(lower, jnp.ones((slots, slots_per), BF16))
    first_v[...] = dot(jnp.ones((8, slots), BF16), lower, NT).astype(jnp.int32)
    place = pltpu.make_async_copy(first_v, first_s, first_sem)
    place.start()
    sums = dot(jnp.concatenate(onehots, axis=0), before)
    taken = jnp.zeros((owners, slots_per), F32)
    named, packed_rows = [], []
    for s in range(subs):
        own = sums[s * owners : (s + 1) * owners]
        rank = jnp.sum(jnp.where(hits[s], own[:, :slots_per] + taken, 0.0), axis=0, keepdims=True)
        start = jnp.sum(jnp.where(hits[s], first, 0.0), axis=0, keepdims=True)
        taken = taken + own[:, slots_per:]
        rank = rank.astype(jnp.int32)
        dead = targets[s] == owners
        within = lax.rem(map_v[s : s + 1, :], 256) + 1
        named.append(jnp.where(id_place == rank, within, 0).astype(F32).astype(BF16))
        slot_ref[s : s + 1, :] = jnp.where(dead, -1, targets[s] * CAP + rank)
        packed_rows.append(jnp.where(dead, -1, start.astype(jnp.int32) + rank))
    table = dot(jnp.concatenate(onehots, axis=1), jnp.concatenate(named, axis=1), NT)
    send_ref[:, blocks * CAP :, :] = jnp.broadcast_to(
        table[:, None, :], (owners, IDROWS, LANES)
    ).astype(BF16)

    for copy in large:
        copy.wait()
    for s in range(subs):
        rest_v[:, s * slots_per : (s + 1) * slots_per] = dot(resid_v[s], basis_v[s]).astype(BF16)

    pick = jnp.where(
        iota((slots, slots), 0) == jnp.concatenate(packed_rows, axis=1), 1.0, 0.0
    ).astype(BF16)
    packed = dot(pick, rest_v[...], NT)
    for q in range(blocks):
        comp_v[q, :slots, :] = packed[:, q * LANES : (q + 1) * LANES]
        comp_v[q, slots:, :] = jnp.zeros((CAP, LANES), F32)
    place.wait()

    for o in range(owners):
        rows = pl.ds(first_s[0, o], CAP)
        for q in range(blocks):
            send_ref[o, q * CAP : (q + 1) * CAP, :] = comp_v[q, rows, :].astype(BF16)


def owner_kernel(recv_ref, inv_ref, back_ref, got_v, match_v, total_v):
    owners, _, rcols = back_ref.shape
    blocks = rcols // LANES
    cblock = inv_ref.shape[0]
    step = LANES // CAP
    wide = OWNER_WIDE
    total_v[...] = jnp.zeros_like(total_v)

    @pl.loop(0, owners // (wide * step))
    def _(t):
        dof = iota((cblock, LANES), 0) + 1
        for u in range(wide):
            mine = pl.ds((t * wide + u) * step, step)
            rows = slice(u * LANES, (u + 1) * LANES)
            named = jnp.sum(recv_ref[mine, blocks * CAP :, :].astype(F32), axis=0)
            named = named[0:1, :].astype(jnp.int32)
            match_v[t, :, rows] = jnp.where(dof == named, 1.0, 0.0).astype(BF16)
            for q in range(blocks):
                got_v[rows, q * LANES : (q + 1) * LANES] = recv_ref[
                    mine, q * CAP : (q + 1) * CAP, :
                ].reshape(LANES, LANES)
        total_v[...] += dot(match_v[t], got_v[...])

    sol = dot(inv_ref[...], total_v[...].astype(BF16)).astype(BF16)

    @pl.loop(0, owners // (wide * step))
    def _(t):
        part = dot(match_v[t], sol, TN).astype(BF16)
        back_ref[pl.ds(t * wide * step, wide * step)] = part.reshape(wide * step, CAP, rcols)


def finish_kernel(
    back_ref, slot_ref, resid_ref, inv_ref, basis_ref, out_hbm, turned_v, row_v, out_v, out_sem
):
    subs, rcols, _ = resid_ref.shape
    slots_per = basis_ref.shape[2]
    rows = back_ref.shape[0] * CAP
    turned_v[...] = back_ref[...].reshape(rows, rcols).T
    batch = FINISH_BATCH
    for s in range(subs):
        row_v[s // batch, :, s % batch * slots_per : (s % batch + 1) * slots_per] = (
            jnp.broadcast_to(slot_ref[s : s + 1, :], (8, slots_per))
        )

    def store(s):
        return pltpu.make_async_copy(out_v.at[s], out_hbm.at[s], out_sem.at[s])

    @pl.loop(0, subs // batch)
    def _(t):
        place = iota((rows, batch * slots_per), 0)
        pick = jnp.where(place == row_v[t, 0:1, :], 1.0, 0.0).astype(BF16)
        pulled = dot(turned_v[...], pick).astype(BF16)
        for i in range(batch):
            s = t * batch + i
            out_v[s] = dot(resid_ref[s], inv_ref[s], NT) + dot(
                pulled[:, i * slots_per : (i + 1) * slots_per], basis_ref[s], NT
            )
            store(s).start()

    for s in range(subs):
        store(s).wait()


ANY = pl.BlockSpec(memory_space=pl.ANY)
HBM = pl.BlockSpec(memory_space=pltpu.HBM)
INVMEM = pl.BlockSpec(memory_space=pltpu.VMEM)
INSMEM = pl.BlockSpec(memory_space=pltpu.SMEM)


def params(mib):
    return pltpu.CompilerParams(vmem_limit_bytes=mib * 1024 * 1024)


def pack(me, counts, cmap, resid, basis, owners):
    subs, rcols, _ = resid.shape
    slots_per = basis.shape[2]
    shape = (owners, rcols // LANES * CAP + IDROWS, LANES)
    return pl.pallas_call(
        pack_kernel,
        out_shape=(
            jax.ShapeDtypeStruct(shape, BF16),
            jax.ShapeDtypeStruct((subs, slots_per), jnp.int32),
        ),
        in_specs=[INSMEM, HBM, HBM, HBM, HBM],
        out_specs=(INVMEM, INVMEM),
        scratch_shapes=[
            pltpu.SMEM(counts.shape, jnp.int32),
            pltpu.VMEM(cmap.shape, jnp.int32),
            pltpu.VMEM(resid.shape, BF16),
            pltpu.VMEM(basis.shape, BF16),
            pltpu.VMEM((rcols, subs * slots_per), BF16),
            pltpu.VMEM((rcols // LANES, subs * slots_per + CAP, LANES), F32),
            pltpu.VMEM((8, owners), jnp.int32),
            pltpu.SMEM((8, owners), jnp.int32),
            pltpu.SemaphoreType.DMA((2,)),
            pltpu.SemaphoreType.DMA((2,)),
            pltpu.SemaphoreType.DMA,
        ],
        compiler_params=params(24),
        name="pack",
    )(me, *[pltpu.with_memory_space_constraint(x, pltpu.HBM) for x in (counts, cmap, resid, basis)])


def owner(recv, inv, rcols):
    owners = recv.shape[0]
    return pl.pallas_call(
        owner_kernel,
        out_shape=jax.ShapeDtypeStruct((owners, CAP, rcols), BF16),
        in_specs=[INVMEM, INVMEM],
        out_specs=INVMEM,
        scratch_shapes=[
            pltpu.VMEM((OWNER_WIDE * LANES, rcols), BF16),
            pltpu.VMEM(
                (owners * CAP // (OWNER_WIDE * LANES), inv.shape[0], OWNER_WIDE * LANES), BF16
            ),
            pltpu.VMEM((inv.shape[0], rcols), F32),
        ],
        compiler_params=params(24),
        name="owner",
    )(recv, inv)


def finish(back, slot, resid, inv, basis):
    subs, rcols, _ = resid.shape
    rows = back.shape[0] * CAP
    return pl.pallas_call(
        finish_kernel,
        out_shape=jax.ShapeDtypeStruct(resid.shape, F32),
        in_specs=[INVMEM] * 5,
        out_specs=ANY,
        scratch_shapes=[
            pltpu.VMEM((rcols, rows), BF16),
            pltpu.VMEM((subs // FINISH_BATCH, 8, FINISH_BATCH * basis.shape[2]), jnp.int32),
            pltpu.VMEM(resid.shape, F32),
            pltpu.SemaphoreType.DMA((subs,)),
        ],
        compiler_params=params(32),
        name="finish",
    )(back, slot, resid, inv, basis)


def per_device(resid, local_inv, basis, coarse_inv, coarse_map, row_counts):
    owners = lax.axis_size("sub") * lax.axis_size("grp")
    me = lax.axis_index(AXES).astype(jnp.int32).reshape(1)
    send, slot = pack(me, row_counts, coarse_map, resid, basis, owners)
    recv = lax.all_to_all(send, AXES, split_axis=0, concat_axis=0, tiled=True)
    back = owner(recv, coarse_inv, resid.shape[1])
    back = lax.all_to_all(back, AXES, split_axis=0, concat_axis=0, tiled=True)
    return finish(back, slot, resid, local_inv, basis)


def solution(mesh):
    placed = (
        P(("sub", "grp"), None, None),
        P(("sub", "grp"), None, None),
        P(("sub", "grp"), None, None),
        P(("sub", "grp"), None),
        P(("sub", "grp"), None),
        P(("sub", "grp")),
    )
    return jax.shard_map(
        per_device,
        mesh=mesh,
        in_specs=placed,
        out_specs=P(("sub", "grp"), None, None),
        check_vma=False,
    )
```

```python
import jax
import jax.numpy as jnp
from jax import lax
from jax.experimental import pallas as pl
from jax.experimental.pallas import tpu as pltpu
from jax.sharding import PartitionSpec as P

CAP = 16
LANES = 128
IDROWS = 4
FINISH_BATCH = 4
F32 = jnp.float32
BF16 = jnp.bfloat16
AXES = ("sub", "grp")
NT = (((1,), (1,)), ((), ()))
TN = (((0,), (0,)), ((), ()))


def iota(shape, axis):
    return lax.broadcasted_iota(jnp.int32, shape, axis)


def dot(a, b, dims=(((1,), (0,)), ((), ()))):
    return lax.dot_general(a, b, dims, preferred_element_type=F32)


def pack_kernel(
    me_ref, counts_hbm, map_hbm, resid_hbm, basis_hbm, send_ref, slot_ref, first_ref,
    counts_v, map_v, resid_v, basis_v, rest_v, comp_v, table_v, first_s, small_sem, in_sem, first_sem,
):
    subs, rcols, _ = resid_hbm.shape
    slots_per = basis_hbm.shape[2]
    slots = subs * slots_per
    owners = send_ref.shape[0]
    blocks = rcols // LANES
    small = (
        pltpu.make_async_copy(map_hbm, map_v, small_sem.at[0]),
        pltpu.make_async_copy(counts_hbm, counts_v, small_sem.at[1]),
    )
    large = (
        pltpu.make_async_copy(basis_hbm, basis_v, in_sem.at[0]),
        pltpu.make_async_copy(resid_hbm, resid_v, in_sem.at[1]),
    )
    for copy in small + large:
        copy.start()
    for copy in small:
        copy.wait()

    lane = iota((1, slots_per), 1)
    row = iota((owners, slots_per), 0)
    before = jnp.where(
        iota((slots_per, 2 * slots_per), 0) < iota((slots_per, 2 * slots_per), 1), 1.0, 0.0
    ).astype(BF16)
    group = lax.rem(me_ref[0], LANES // CAP)
    id_row = iota((LANES, slots_per), 0)
    id_place = jnp.where(id_row // CAP == group, lax.rem(id_row, CAP), -1)
    targets = [
        jnp.where(lane < counts_v[s], map_v[s : s + 1, :] // 256, owners) for s in range(subs)
    ]
    hits = [row == target for target in targets]
    onehots = [jnp.where(hit, 1.0, 0.0).astype(BF16) for hit in hits]
    lower = jnp.concatenate(
        [jnp.where(row > target, 1.0, 0.0).astype(BF16) for target in targets], axis=1
    )
    first = dot(lower, jnp.ones((slots, slots_per), BF16))
    first_ref[...] = dot(jnp.ones((8, slots), BF16), lower, NT).astype(jnp.int32)
    place = pltpu.make_async_copy(first_ref, first_s, first_sem)
    place.start()
    sums = dot(jnp.concatenate(onehots, axis=0), before)
    taken = jnp.zeros((owners, slots_per), F32)
    named, packed_rows = [], []
    for s in range(subs):
        own = sums[s * owners : (s + 1) * owners]
        rank = jnp.sum(jnp.where(hits[s], own[:, :slots_per] + taken, 0.0), axis=0, keepdims=True)
        start = jnp.sum(jnp.where(hits[s], first, 0.0), axis=0, keepdims=True)
        taken = taken + own[:, slots_per:]
        rank = rank.astype(jnp.int32)
        dead = targets[s] == owners
        within = lax.rem(map_v[s : s + 1, :], 256) + 1
        named.append(jnp.where(id_place == rank, within, 0).astype(F32).astype(BF16))
        packed_rows.append(jnp.where(dead, -1, start.astype(jnp.int32) + rank))
        slot_ref[s : s + 1, :] = packed_rows[s]
    table = dot(jnp.concatenate(onehots, axis=1), jnp.concatenate(named, axis=1), NT)
    chunk = blocks * CAP + IDROWS
    sent = send_ref.reshape(owners * chunk, LANES)
    table_v[:owners, :] = table
    table_v[owners:, :] = jnp.zeros((8, LANES), F32)
    for o in range(owners):
        sent[o * chunk + blocks * CAP : (o + 1) * chunk, :] = table_v[o : o + IDROWS, :].astype(
            BF16
        )

    for copy in large:
        copy.wait()
    for s in range(subs):
        rest_v[:, s * slots_per : (s + 1) * slots_per] = dot(resid_v[s], basis_v[s]).astype(BF16)

    pick = jnp.where(
        iota((slots, slots), 0) == jnp.concatenate(packed_rows, axis=1), 1.0, 0.0
    ).astype(BF16)
    packed = dot(pick, rest_v[...], NT)
    for q in range(blocks):
        comp_v[q, :slots, :] = packed[:, q * LANES : (q + 1) * LANES]
        comp_v[q, slots:, :] = jnp.zeros((CAP, LANES), F32)
    place.wait()

    for o in range(owners):
        rows = pl.ds(first_s[0, o], CAP)
        for q in range(blocks):
            here = o * chunk + q * CAP
            sent[here : here + CAP, :] = comp_v[q, rows, :].astype(BF16)


def owner_kernel(recv_ref, inv_ref, back_ref, got_v, match_v):
    owners, _, rcols = back_ref.shape
    blocks = rcols // LANES
    cblock = inv_ref.shape[0]
    step = LANES // CAP
    chunk = blocks * CAP + IDROWS
    recv = recv_ref.reshape(owners * chunk, LANES)
    dof = iota((cblock, LANES), 0) + 1
    for t in range(owners // step):
        rows = slice(t * LANES, (t + 1) * LANES)
        named = jnp.zeros((IDROWS, LANES), BF16)
        for d in range(t * step, (t + 1) * step):
            named = named + recv[d * chunk + blocks * CAP : (d + 1) * chunk, :]
            for q in range(blocks):
                here = d * chunk + q * CAP
                got_v[d * CAP : (d + 1) * CAP, q * LANES : (q + 1) * LANES] = recv[
                    here : here + CAP, :
                ]
        named = named[0:1, :].astype(F32).astype(jnp.int32)
        match_v[:, rows] = jnp.where(dof == named, 1.0, 0.0).astype(BF16)
    total = dot(match_v[...], got_v[...])
    sol = dot(inv_ref[...], total.astype(BF16)).astype(BF16)
    part = dot(match_v[...], sol, TN).astype(BF16)
    back_ref[...] = part.reshape(owners, CAP, rcols)


def finish_kernel(
    back_ref, slot_ref, first_ref, resid_ref, inv_ref, basis_ref, out_hbm,
    first_s, comp_v, turned_v, out_v, first_sem, out_sem,
):
    subs, rcols, _ = resid_ref.shape
    slots_per = basis_ref.shape[2]
    slots = subs * slots_per
    owners = back_ref.shape[0]
    blocks = rcols // LANES
    place = pltpu.make_async_copy(first_ref, first_s, first_sem)
    place.start()
    comp_v[...] = jnp.zeros_like(comp_v)
    for s in range(subs):
        out_v[s] = dot(resid_ref[s], inv_ref[s], NT)
    place.wait()

    for o in range(owners):
        rows = pl.ds(first_s[0, o], CAP)
        for q in range(blocks):
            comp_v[q, rows, :] = back_ref[o, :, q * LANES : (q + 1) * LANES].astype(F32)
    for q in range(blocks):
        turned_v[q * LANES : (q + 1) * LANES, :] = comp_v[q, :slots, :].astype(BF16).T
    stores = []
    for first in range(0, subs, FINISH_BATCH):
        chosen = range(first, first + FINISH_BATCH)
        packed = jnp.concatenate([slot_ref[s : s + 1, :] for s in chosen], axis=1)
        pick = jnp.where(iota((slots, packed.shape[1]), 0) == packed, 1.0, 0.0).astype(BF16)
        pulled = dot(turned_v[...], pick).astype(BF16)
        for i, s in enumerate(chosen):
            out_v[s] = out_v[s] + dot(
                pulled[:, i * slots_per : (i + 1) * slots_per], basis_ref[s], NT
            )
            copy = pltpu.make_async_copy(out_v.at[s], out_hbm.at[s], out_sem.at[s])
            copy.start()
            stores.append(copy)
    for copy in stores:
        copy.wait()


ANY = pl.BlockSpec(memory_space=pl.ANY)
HBM = pl.BlockSpec(memory_space=pltpu.HBM)
INVMEM = pl.BlockSpec(memory_space=pltpu.VMEM)
INSMEM = pl.BlockSpec(memory_space=pltpu.SMEM)


def params(mib):
    return pltpu.CompilerParams(vmem_limit_bytes=mib * 1024 * 1024)


def pack(me, counts, cmap, resid, basis, owners):
    subs, rcols, _ = resid.shape
    slots_per = basis.shape[2]
    shape = (owners, (rcols // LANES * CAP + IDROWS) // IDROWS, IDROWS, LANES)
    return pl.pallas_call(
        pack_kernel,
        out_shape=(
            jax.ShapeDtypeStruct(shape, BF16),
            jax.ShapeDtypeStruct((subs, slots_per), jnp.int32),
            jax.ShapeDtypeStruct((8, owners), jnp.int32),
        ),
        in_specs=[INSMEM, HBM, HBM, HBM, HBM],
        out_specs=(INVMEM, INVMEM, INVMEM),
        scratch_shapes=[
            pltpu.SMEM(counts.shape, jnp.int32),
            pltpu.VMEM(cmap.shape, jnp.int32),
            pltpu.VMEM(resid.shape, BF16),
            pltpu.VMEM(basis.shape, BF16),
            pltpu.VMEM((rcols, subs * slots_per), BF16),
            pltpu.VMEM((rcols // LANES, subs * slots_per + CAP, LANES), F32),
            pltpu.VMEM((owners + 8, LANES), F32),
            pltpu.SMEM((8, owners), jnp.int32),
            pltpu.SemaphoreType.DMA((2,)),
            pltpu.SemaphoreType.DMA((2,)),
            pltpu.SemaphoreType.DMA,
        ],
        compiler_params=params(24),
        name="pack",
    )(me, *[pltpu.with_memory_space_constraint(x, pltpu.HBM) for x in (counts, cmap, resid, basis)])


def owner(recv, inv, rcols):
    owners = recv.shape[0]
    return pl.pallas_call(
        owner_kernel,
        out_shape=jax.ShapeDtypeStruct((owners, CAP, rcols), BF16),
        in_specs=[INVMEM, INVMEM],
        out_specs=INVMEM,
        scratch_shapes=[
            pltpu.VMEM((owners * CAP, rcols), BF16),
            pltpu.VMEM((inv.shape[0], owners * CAP), BF16),
        ],
        compiler_params=params(24),
        name="owner",
    )(recv, inv)


def finish(back, slot, first, resid, inv, basis):
    subs, rcols, _ = resid.shape
    slots = slot.size
    return pl.pallas_call(
        finish_kernel,
        out_shape=jax.ShapeDtypeStruct(resid.shape, F32),
        in_specs=[INVMEM] * 6,
        out_specs=ANY,
        scratch_shapes=[
            pltpu.SMEM(first.shape, jnp.int32),
            pltpu.VMEM((rcols // LANES, slots + CAP, LANES), F32),
            pltpu.VMEM((rcols, slots), BF16),
            pltpu.VMEM(resid.shape, F32),
            pltpu.SemaphoreType.DMA,
            pltpu.SemaphoreType.DMA((subs,)),
        ],
        compiler_params=params(32),
        name="finish",
    )(back, slot, first, resid, inv, basis)


def per_device(resid, local_inv, basis, coarse_inv, coarse_map, row_counts):
    owners = lax.axis_size("sub") * lax.axis_size("grp")
    me = lax.axis_index(AXES).astype(jnp.int32).reshape(1)
    send, slot, first = pack(me, row_counts, coarse_map, resid, basis, owners)
    recv = lax.all_to_all(send, AXES, split_axis=0, concat_axis=0, tiled=True)
    back = owner(recv, coarse_inv, resid.shape[1])
    back = lax.all_to_all(back, AXES, split_axis=0, concat_axis=0, tiled=True)
    return finish(back, slot, first, resid, local_inv, basis)


def solution(mesh):
    placed = (
        P(("sub", "grp"), None, None),
        P(("sub", "grp"), None, None),
        P(("sub", "grp"), None, None),
        P(("sub", "grp"), None),
        P(("sub", "grp"), None),
        P(("sub", "grp")),
    )
    return jax.shard_map(
        per_device,
        mesh=mesh,
        in_specs=placed,
        out_specs=P(("sub", "grp"), None, None),
        check_vma=False,
    )
```

```python
import jax
import jax.numpy as jnp
from jax import lax
from jax.experimental import pallas as pl
from jax.experimental.pallas import tpu as pltpu
from jax.sharding import PartitionSpec as P

CAP = 16
LANES = 128
IDROWS = 4
FINISH_BATCH = 4
F32 = jnp.float32
BF16 = jnp.bfloat16
AXES = ("sub", "grp")
NT = (((1,), (1,)), ((), ()))
TN = (((0,), (0,)), ((), ()))


def iota(shape, axis):
    return lax.broadcasted_iota(jnp.int32, shape, axis)


def dot(a, b, dims=(((1,), (0,)), ((), ()))):
    return lax.dot_general(a, b, dims, preferred_element_type=F32)


def pack_kernel(
    counts_hbm, map_hbm, resid_hbm, basis_hbm, send_ref, slot_ref, first_ref,
    counts_v, map_v, resid_v, basis_v, rest_v, comp_v, table_v, first_s, small_sem, in_sem, first_sem,
):
    subs, rcols, _ = resid_hbm.shape
    slots_per = basis_hbm.shape[2]
    slots = subs * slots_per
    owners = send_ref.shape[0]
    blocks = rcols // LANES
    small = (
        pltpu.make_async_copy(map_hbm, map_v, small_sem.at[0]),
        pltpu.make_async_copy(counts_hbm, counts_v, small_sem.at[1]),
    )
    large = (
        pltpu.make_async_copy(basis_hbm, basis_v, in_sem.at[0]),
        pltpu.make_async_copy(resid_hbm, resid_v, in_sem.at[1]),
    )
    for copy in small + large:
        copy.start()
    for copy in small:
        copy.wait()

    lane = iota((1, slots_per), 1)
    row = iota((owners, slots_per), 0)
    before = jnp.where(
        iota((slots_per, 2 * slots_per), 0) < iota((slots_per, 2 * slots_per), 1), 1.0, 0.0
    ).astype(BF16)
    id_place = lax.rem(iota((LANES, slots_per), 0), CAP)
    targets = [
        jnp.where(lane < counts_v[s], map_v[s : s + 1, :] // 256, owners) for s in range(subs)
    ]
    hits = [row == target for target in targets]
    onehots = [jnp.where(hit, 1.0, 0.0).astype(BF16) for hit in hits]
    lower = jnp.concatenate(
        [jnp.where(row > target, 1.0, 0.0).astype(BF16) for target in targets], axis=1
    )
    first = dot(lower, jnp.ones((slots, slots_per), BF16))
    first_ref[...] = dot(jnp.ones((8, slots), BF16), lower, NT).astype(jnp.int32)
    place = pltpu.make_async_copy(first_ref, first_s, first_sem)
    place.start()
    sums = dot(jnp.concatenate(onehots, axis=0), before)
    taken = jnp.zeros((owners, slots_per), F32)
    named, packed_rows = [], []
    for s in range(subs):
        own = sums[s * owners : (s + 1) * owners]
        rank = jnp.sum(jnp.where(hits[s], own[:, :slots_per] + taken, 0.0), axis=0, keepdims=True)
        start = jnp.sum(jnp.where(hits[s], first, 0.0), axis=0, keepdims=True)
        taken = taken + own[:, slots_per:]
        rank = rank.astype(jnp.int32)
        dead = targets[s] == owners
        within = lax.rem(map_v[s : s + 1, :], 256) + 1
        named.append(jnp.where(id_place == rank, within, 0).astype(F32).astype(BF16))
        packed_rows.append(jnp.where(dead, -1, start.astype(jnp.int32) + rank))
        slot_ref[s : s + 1, :] = packed_rows[s]
    table = dot(jnp.concatenate(onehots, axis=1), jnp.concatenate(named, axis=1), NT)
    chunk = blocks * CAP + IDROWS
    sent = send_ref.reshape(owners * chunk, LANES)
    table_v[:owners, :] = table
    table_v[owners:, :] = jnp.zeros((8, LANES), F32)
    for o in range(owners):
        sent[o * chunk + blocks * CAP : (o + 1) * chunk, :] = table_v[o : o + IDROWS, :].astype(
            BF16
        )

    for copy in large:
        copy.wait()
    for s in range(subs):
        rest_v[:, s * slots_per : (s + 1) * slots_per] = dot(resid_v[s], basis_v[s]).astype(BF16)

    pick = jnp.where(
        iota((slots, slots), 0) == jnp.concatenate(packed_rows, axis=1), 1.0, 0.0
    ).astype(BF16)
    packed = dot(pick, rest_v[...], NT)
    for q in range(blocks):
        comp_v[q, :slots, :] = packed[:, q * LANES : (q + 1) * LANES]
        comp_v[q, slots:, :] = jnp.zeros((CAP, LANES), F32)
    place.wait()

    for o in range(owners):
        rows = pl.ds(first_s[0, o], CAP)
        for q in range(blocks):
            here = o * chunk + q * CAP
            sent[here : here + CAP, :] = comp_v[q, rows, :].astype(BF16)


def owner_kernel(recv_ref, inv_ref, back_ref, got_v, match_v):
    owners, _, rcols = back_ref.shape
    blocks = rcols // LANES
    cblock = inv_ref.shape[0]
    step = LANES // CAP
    chunk = blocks * CAP + IDROWS
    recv = recv_ref.reshape(owners * chunk, LANES)
    dof = iota((cblock, LANES), 0) + 1
    part_of = iota((IDROWS, LANES), 1) // CAP
    for t in range(owners // step):
        rows = slice(t * LANES, (t + 1) * LANES)
        named = jnp.zeros((IDROWS, LANES), BF16)
        for d in range(t * step, (t + 1) * step):
            ids = recv[d * chunk + blocks * CAP : (d + 1) * chunk, :]
            named = jnp.where(part_of == d % step, ids, named)
            for q in range(blocks):
                here = d * chunk + q * CAP
                got_v[d * CAP : (d + 1) * CAP, q * LANES : (q + 1) * LANES] = recv[
                    here : here + CAP, :
                ]
        named = named[0:1, :].astype(F32).astype(jnp.int32)
        match_v[:, rows] = jnp.where(dof == named, 1.0, 0.0).astype(BF16)
    total = dot(match_v[...], got_v[...])
    sol = dot(inv_ref[...], total.astype(BF16)).astype(BF16)
    part = dot(match_v[...], sol, TN).astype(BF16)
    back_ref[...] = part.reshape(owners, CAP, rcols)


def finish_kernel(
    back_ref, slot_ref, first_ref, resid_ref, inv_ref, basis_ref, out_hbm,
    comp_v, turned_v, out_v, out_sem,
):
    subs, rcols, _ = resid_ref.shape
    slots_per = basis_ref.shape[2]
    slots = subs * slots_per
    owners = back_ref.shape[0]
    blocks = rcols // LANES
    starts = first_ref[0:1, :]
    comp_v[...] = jnp.zeros_like(comp_v)
    for s in range(subs):
        out_v[s] = dot(resid_ref[s], inv_ref[s], NT)

    for o in range(owners):
        rows = pl.ds(starts[0, o], CAP)
        for q in range(blocks):
            comp_v[q, rows, :] = back_ref[o, :, q * LANES : (q + 1) * LANES].astype(F32)
    for q in range(blocks):
        turned_v[q * LANES : (q + 1) * LANES, :] = comp_v[q, :slots, :].astype(BF16).T
    stores = []
    for first in range(0, subs, FINISH_BATCH):
        chosen = range(first, first + FINISH_BATCH)
        packed = jnp.concatenate([slot_ref[s : s + 1, :] for s in chosen], axis=1)
        pick = jnp.where(iota((slots, packed.shape[1]), 0) == packed, 1.0, 0.0).astype(BF16)
        pulled = dot(turned_v[...], pick).astype(BF16)
        for i, s in enumerate(chosen):
            out_v[s] = out_v[s] + dot(
                pulled[:, i * slots_per : (i + 1) * slots_per], basis_ref[s], NT
            )
            copy = pltpu.make_async_copy(out_v.at[s], out_hbm.at[s], out_sem.at[s])
            copy.start()
            stores.append(copy)
    for copy in stores:
        copy.wait()


ANY = pl.BlockSpec(memory_space=pl.ANY)
HBM = pl.BlockSpec(memory_space=pltpu.HBM)
INVMEM = pl.BlockSpec(memory_space=pltpu.VMEM)


def params(mib):
    return pltpu.CompilerParams(vmem_limit_bytes=mib * 1024 * 1024)


def pack(counts, cmap, resid, basis, owners):
    subs, rcols, _ = resid.shape
    slots_per = basis.shape[2]
    shape = (owners, (rcols // LANES * CAP + IDROWS) // IDROWS, IDROWS, LANES)
    return pl.pallas_call(
        pack_kernel,
        out_shape=(
            jax.ShapeDtypeStruct(shape, BF16),
            jax.ShapeDtypeStruct((subs, slots_per), jnp.int32),
            jax.ShapeDtypeStruct((8, owners), jnp.int32),
        ),
        in_specs=[HBM, HBM, HBM, HBM],
        out_specs=(INVMEM, INVMEM, INVMEM),
        scratch_shapes=[
            pltpu.SMEM(counts.shape, jnp.int32),
            pltpu.VMEM(cmap.shape, jnp.int32),
            pltpu.VMEM(resid.shape, BF16),
            pltpu.VMEM(basis.shape, BF16),
            pltpu.VMEM((rcols, subs * slots_per), BF16),
            pltpu.VMEM((rcols // LANES, subs * slots_per + CAP, LANES), F32),
            pltpu.VMEM((owners + 8, LANES), F32),
            pltpu.SMEM((8, owners), jnp.int32),
            pltpu.SemaphoreType.DMA((2,)),
            pltpu.SemaphoreType.DMA((2,)),
            pltpu.SemaphoreType.DMA,
        ],
        compiler_params=params(24),
        name="pack",
    )(*[pltpu.with_memory_space_constraint(x, pltpu.HBM) for x in (counts, cmap, resid, basis)])


def owner(recv, inv, rcols):
    owners = recv.shape[0]
    return pl.pallas_call(
        owner_kernel,
        out_shape=jax.ShapeDtypeStruct((owners, CAP, rcols), BF16),
        in_specs=[INVMEM, INVMEM],
        out_specs=INVMEM,
        scratch_shapes=[
            pltpu.VMEM((owners * CAP, rcols), BF16),
            pltpu.VMEM((inv.shape[0], owners * CAP), BF16),
        ],
        compiler_params=params(24),
        name="owner",
    )(recv, inv)


def finish(back, slot, first, resid, inv, basis):
    subs, rcols, _ = resid.shape
    slots = slot.size
    return pl.pallas_call(
        finish_kernel,
        out_shape=jax.ShapeDtypeStruct(resid.shape, F32),
        in_specs=[INVMEM] * 6,
        out_specs=ANY,
        scratch_shapes=[
            pltpu.VMEM((rcols // LANES, slots + CAP, LANES), F32),
            pltpu.VMEM((rcols, slots), BF16),
            pltpu.VMEM(resid.shape, F32),
            pltpu.SemaphoreType.DMA((subs,)),
        ],
        compiler_params=params(32),
        name="finish",
    )(back, slot, first, resid, inv, basis)


def per_device(resid, local_inv, basis, coarse_inv, coarse_map, row_counts):
    owners = lax.axis_size("sub") * lax.axis_size("grp")
    send, slot, first = pack(row_counts, coarse_map, resid, basis, owners)
    recv = lax.all_to_all(send, AXES, split_axis=0, concat_axis=0, tiled=True)
    back = owner(recv, coarse_inv, resid.shape[1])
    back = lax.all_to_all(back, AXES, split_axis=0, concat_axis=0, tiled=True)
    return finish(back, slot, first, resid, local_inv, basis)


def solution(mesh):
    placed = (
        P(("sub", "grp"), None, None),
        P(("sub", "grp"), None, None),
        P(("sub", "grp"), None, None),
        P(("sub", "grp"), None),
        P(("sub", "grp"), None),
        P(("sub", "grp")),
    )
    return jax.shard_map(
        per_device,
        mesh=mesh,
        in_specs=placed,
        out_specs=P(("sub", "grp"), None, None),
        check_vma=False,
    )
```

```python
import jax
import jax.numpy as jnp
from jax import lax
from jax.experimental import pallas as pl
from jax.experimental.pallas import tpu as pltpu
from jax.sharding import PartitionSpec as P

CAP = 16
LANES = 128
IDROWS = 4
FINISH_BATCH = 4
F32 = jnp.float32
BF16 = jnp.bfloat16
AXES = ("sub", "grp")
NT = (((1,), (1,)), ((), ()))
TN = (((0,), (0,)), ((), ()))


def iota(shape, axis):
    return lax.broadcasted_iota(jnp.int32, shape, axis)


def dot(a, b, dims=(((1,), (0,)), ((), ()))):
    return lax.dot_general(a, b, dims, preferred_element_type=F32)


def pack_kernel(
    counts_hbm, map_hbm, resid_hbm, basis_hbm, send_ref, slot_ref, first_ref,
    counts_v, map_v, resid_v, basis_v, rest_v, comp_v, table_v, small_sem, in_sem,
):
    subs, rcols, _ = resid_hbm.shape
    slots_per = basis_hbm.shape[2]
    slots = subs * slots_per
    owners = send_ref.shape[0]
    blocks = rcols // LANES
    small = (
        pltpu.make_async_copy(map_hbm, map_v, small_sem.at[0]),
        pltpu.make_async_copy(counts_hbm, counts_v, small_sem.at[1]),
    )
    large = (
        pltpu.make_async_copy(basis_hbm, basis_v, in_sem.at[0]),
        pltpu.make_async_copy(resid_hbm, resid_v, in_sem.at[1]),
    )
    for copy in small + large:
        copy.start()
    for copy in small:
        copy.wait()

    lane = iota((1, slots_per), 1)
    row = iota((owners, slots_per), 0)
    before = jnp.where(
        iota((slots_per, 2 * slots_per), 0) < iota((slots_per, 2 * slots_per), 1), 1.0, 0.0
    ).astype(BF16)
    id_place = lax.rem(iota((LANES, slots_per), 0), CAP)
    targets = [
        jnp.where(lane < counts_v[s], map_v[s : s + 1, :] // 256, owners) for s in range(subs)
    ]
    hits = [row == target for target in targets]
    onehots = [jnp.where(hit, 1.0, 0.0).astype(BF16) for hit in hits]
    lower = jnp.concatenate(
        [jnp.where(row > target, 1.0, 0.0).astype(BF16) for target in targets], axis=1
    )
    first = dot(lower, jnp.ones((slots, slots_per), BF16))
    first_ref[...] = dot(jnp.ones((8, slots), BF16), lower, NT).astype(jnp.int32)
    sums = dot(jnp.concatenate(onehots, axis=0), before)
    taken = jnp.zeros((owners, slots_per), F32)
    named, packed_rows = [], []
    for s in range(subs):
        own = sums[s * owners : (s + 1) * owners]
        rank = jnp.sum(jnp.where(hits[s], own[:, :slots_per] + taken, 0.0), axis=0, keepdims=True)
        start = jnp.sum(jnp.where(hits[s], first, 0.0), axis=0, keepdims=True)
        taken = taken + own[:, slots_per:]
        rank = rank.astype(jnp.int32)
        dead = targets[s] == owners
        within = lax.rem(map_v[s : s + 1, :], 256) + 1
        named.append(jnp.where(id_place == rank, within, 0).astype(F32).astype(BF16))
        packed_rows.append(jnp.where(dead, -1, start.astype(jnp.int32) + rank))
        slot_ref[s : s + 1, :] = packed_rows[s]
    table = dot(jnp.concatenate(onehots, axis=1), jnp.concatenate(named, axis=1), NT)
    chunk = blocks * CAP + IDROWS
    sent = send_ref.reshape(owners * chunk, LANES)
    table_v[:owners, :] = table
    table_v[owners:, :] = jnp.zeros((8, LANES), F32)
    for o in range(owners):
        sent[o * chunk + blocks * CAP : (o + 1) * chunk, :] = table_v[o : o + IDROWS, :].astype(
            BF16
        )

    for copy in large:
        copy.wait()
    for s in range(subs):
        rest_v[:, s * slots_per : (s + 1) * slots_per] = dot(resid_v[s], basis_v[s]).astype(BF16)

    pick = jnp.where(
        iota((slots, slots), 0) == jnp.concatenate(packed_rows, axis=1), 1.0, 0.0
    ).astype(BF16)
    packed = dot(pick, rest_v[...], NT)
    for q in range(blocks):
        comp_v[q, :slots, :] = packed[:, q * LANES : (q + 1) * LANES]
        comp_v[q, slots:, :] = jnp.zeros((CAP, LANES), F32)

    starts = first_ref[0:1, :]
    for o in range(owners):
        rows = pl.ds(starts[0, o], CAP)
        for q in range(blocks):
            here = o * chunk + q * CAP
            sent[here : here + CAP, :] = comp_v[q, rows, :].astype(BF16)


def owner_kernel(recv_ref, inv_ref, back_ref, got_v, match_v):
    owners, _, rcols = back_ref.shape
    blocks = rcols // LANES
    cblock = inv_ref.shape[0]
    step = LANES // CAP
    chunk = blocks * CAP + IDROWS
    recv = recv_ref.reshape(owners * chunk, LANES)
    dof = iota((cblock, LANES), 0) + 1
    part_of = iota((IDROWS, LANES), 1) // CAP
    for t in range(owners // step):
        rows = slice(t * LANES, (t + 1) * LANES)
        named = jnp.zeros((IDROWS, LANES), BF16)
        for d in range(t * step, (t + 1) * step):
            ids = recv[d * chunk + blocks * CAP : (d + 1) * chunk, :]
            named = jnp.where(part_of == d % step, ids, named)
            for q in range(blocks):
                here = d * chunk + q * CAP
                got_v[d * CAP : (d + 1) * CAP, q * LANES : (q + 1) * LANES] = recv[
                    here : here + CAP, :
                ]
        named = named[0:1, :].astype(F32).astype(jnp.int32)
        match_v[:, rows] = jnp.where(dof == named, 1.0, 0.0).astype(BF16)
    total = dot(match_v[...], got_v[...])
    sol = dot(inv_ref[...], total.astype(BF16)).astype(BF16)
    part = dot(match_v[...], sol, TN).astype(BF16)
    back_ref[...] = part.reshape(owners, CAP, rcols)


def finish_kernel(
    back_ref, slot_ref, first_ref, resid_ref, inv_ref, basis_ref, out_hbm,
    comp_v, turned_v, out_v, out_sem,
):
    subs, rcols, _ = resid_ref.shape
    slots_per = basis_ref.shape[2]
    slots = subs * slots_per
    owners = back_ref.shape[0]
    blocks = rcols // LANES
    starts = first_ref[0:1, :]
    comp_v[...] = jnp.zeros_like(comp_v)
    for s in range(subs):
        out_v[s] = dot(resid_ref[s], inv_ref[s], NT)

    for o in range(owners):
        rows = pl.ds(starts[0, o], CAP)
        for q in range(blocks):
            comp_v[q, rows, :] = back_ref[o, :, q * LANES : (q + 1) * LANES].astype(F32)
    for q in range(blocks):
        turned_v[q * LANES : (q + 1) * LANES, :] = comp_v[q, :slots, :].astype(BF16).T
    stores = []
    for first in range(0, subs, FINISH_BATCH):
        chosen = range(first, first + FINISH_BATCH)
        packed = jnp.concatenate([slot_ref[s : s + 1, :] for s in chosen], axis=1)
        pick = jnp.where(iota((slots, packed.shape[1]), 0) == packed, 1.0, 0.0).astype(BF16)
        pulled = dot(turned_v[...], pick).astype(BF16)
        for i, s in enumerate(chosen):
            out_v[s] = out_v[s] + dot(
                pulled[:, i * slots_per : (i + 1) * slots_per], basis_ref[s], NT
            )
            copy = pltpu.make_async_copy(out_v.at[s], out_hbm.at[s], out_sem.at[s])
            copy.start()
            stores.append(copy)
    for copy in stores:
        copy.wait()


ANY = pl.BlockSpec(memory_space=pl.ANY)
HBM = pl.BlockSpec(memory_space=pltpu.HBM)
INVMEM = pl.BlockSpec(memory_space=pltpu.VMEM)


def params(mib):
    return pltpu.CompilerParams(vmem_limit_bytes=mib * 1024 * 1024)


def pack(counts, cmap, resid, basis, owners):
    subs, rcols, _ = resid.shape
    slots_per = basis.shape[2]
    shape = (owners, (rcols // LANES * CAP + IDROWS) // IDROWS, IDROWS, LANES)
    return pl.pallas_call(
        pack_kernel,
        out_shape=(
            jax.ShapeDtypeStruct(shape, BF16),
            jax.ShapeDtypeStruct((subs, slots_per), jnp.int32),
            jax.ShapeDtypeStruct((8, owners), jnp.int32),
        ),
        in_specs=[HBM, HBM, HBM, HBM],
        out_specs=(INVMEM, INVMEM, INVMEM),
        scratch_shapes=[
            pltpu.SMEM(counts.shape, jnp.int32),
            pltpu.VMEM(cmap.shape, jnp.int32),
            pltpu.VMEM(resid.shape, BF16),
            pltpu.VMEM(basis.shape, BF16),
            pltpu.VMEM((rcols, subs * slots_per), BF16),
            pltpu.VMEM((rcols // LANES, subs * slots_per + CAP, LANES), F32),
            pltpu.VMEM((owners + 8, LANES), F32),
            pltpu.SemaphoreType.DMA((2,)),
            pltpu.SemaphoreType.DMA((2,)),
        ],
        compiler_params=params(24),
        name="pack",
    )(*[pltpu.with_memory_space_constraint(x, pltpu.HBM) for x in (counts, cmap, resid, basis)])


def owner(recv, inv, rcols):
    owners = recv.shape[0]
    return pl.pallas_call(
        owner_kernel,
        out_shape=jax.ShapeDtypeStruct((owners, CAP, rcols), BF16),
        in_specs=[INVMEM, INVMEM],
        out_specs=INVMEM,
        scratch_shapes=[
            pltpu.VMEM((owners * CAP, rcols), BF16),
            pltpu.VMEM((inv.shape[0], owners * CAP), BF16),
        ],
        compiler_params=params(24),
        name="owner",
    )(recv, inv)


def finish(back, slot, first, resid, inv, basis):
    subs, rcols, _ = resid.shape
    slots = slot.size
    return pl.pallas_call(
        finish_kernel,
        out_shape=jax.ShapeDtypeStruct(resid.shape, F32),
        in_specs=[INVMEM] * 6,
        out_specs=ANY,
        scratch_shapes=[
            pltpu.VMEM((rcols // LANES, slots + CAP, LANES), F32),
            pltpu.VMEM((rcols, slots), BF16),
            pltpu.VMEM(resid.shape, F32),
            pltpu.SemaphoreType.DMA((subs,)),
        ],
        compiler_params=params(32),
        name="finish",
    )(back, slot, first, resid, inv, basis)


def per_device(resid, local_inv, basis, coarse_inv, coarse_map, row_counts):
    owners = lax.axis_size("sub") * lax.axis_size("grp")
    send, slot, first = pack(row_counts, coarse_map, resid, basis, owners)
    recv = lax.all_to_all(send, AXES, split_axis=0, concat_axis=0, tiled=True)
    back = owner(recv, coarse_inv, resid.shape[1])
    back = lax.all_to_all(back, AXES, split_axis=0, concat_axis=0, tiled=True)
    return finish(back, slot, first, resid, local_inv, basis)


def solution(mesh):
    placed = (
        P(("sub", "grp"), None, None),
        P(("sub", "grp"), None, None),
        P(("sub", "grp"), None, None),
        P(("sub", "grp"), None),
        P(("sub", "grp"), None),
        P(("sub", "grp")),
    )
    return jax.shard_map(
        per_device,
        mesh=mesh,
        in_specs=placed,
        out_specs=P(("sub", "grp"), None, None),
        check_vma=False,
    )
```

```python
import jax
import jax.numpy as jnp
from jax import lax
from jax.experimental import pallas as pl
from jax.experimental.pallas import tpu as pltpu
from jax.sharding import PartitionSpec as P

CAP = 16
LANES = 128
IDROWS = 4
FINISH_BATCH = 4
F32 = jnp.float32
BF16 = jnp.bfloat16
AXES = ("sub", "grp")
NT = (((1,), (1,)), ((), ()))
TN = (((0,), (0,)), ((), ()))


def iota(shape, axis):
    return lax.broadcasted_iota(jnp.int32, shape, axis)


def dot(a, b, dims=(((1,), (0,)), ((), ()))):
    return lax.dot_general(a, b, dims, preferred_element_type=F32)


def pack_kernel(
    counts_hbm, map_hbm, resid_hbm, basis_hbm, send_ref, slot_ref, first_ref,
    counts_v, map_v, resid_v, basis_v, rest_v, comp_v, table_v, small_sem, in_sem,
):
    subs, rcols, _ = resid_hbm.shape
    slots_per = basis_hbm.shape[2]
    slots = subs * slots_per
    owners = send_ref.shape[0]
    blocks = rcols // LANES
    small = (
        pltpu.make_async_copy(map_hbm, map_v, small_sem.at[0]),
        pltpu.make_async_copy(counts_hbm, counts_v, small_sem.at[1]),
    )
    large = (
        pltpu.make_async_copy(basis_hbm, basis_v, in_sem.at[0]),
        pltpu.make_async_copy(resid_hbm, resid_v, in_sem.at[1]),
    )
    for copy in small + large:
        copy.start()
    for copy in small:
        copy.wait()

    lane = iota((1, slots_per), 1)
    row = iota((owners, slots_per), 0)
    before = jnp.where(
        iota((slots_per, 2 * slots_per), 0) < iota((slots_per, 2 * slots_per), 1), 1.0, 0.0
    ).astype(BF16)
    id_place = lax.rem(iota((LANES, slots_per), 0), CAP)
    targets = [
        jnp.where(lane < counts_v[s], map_v[s : s + 1, :] // 256, owners) for s in range(subs)
    ]
    hits = [row == target for target in targets]
    onehots = [jnp.where(hit, 1.0, 0.0).astype(BF16) for hit in hits]
    lower = jnp.concatenate(
        [jnp.where(row > target, 1.0, 0.0).astype(BF16) for target in targets], axis=1
    )
    first = dot(lower, jnp.ones((slots, slots_per), BF16))
    first_ref[...] = dot(jnp.ones((8, slots), BF16), lower, NT).astype(jnp.int32)
    sums = dot(jnp.concatenate(onehots, axis=0), before)
    taken = jnp.zeros((owners, slots_per), F32)
    named, packed_rows = [], []
    for s in range(subs):
        own = sums[s * owners : (s + 1) * owners]
        rank = jnp.sum(jnp.where(hits[s], own[:, :slots_per] + taken, 0.0), axis=0, keepdims=True)
        start = jnp.sum(jnp.where(hits[s], first, 0.0), axis=0, keepdims=True)
        taken = taken + own[:, slots_per:]
        rank = rank.astype(jnp.int32)
        dead = targets[s] == owners
        within = lax.rem(map_v[s : s + 1, :], 256) + 1
        named.append(jnp.where(id_place == rank, within, 0).astype(F32).astype(BF16))
        packed_rows.append(jnp.where(dead, -1, start.astype(jnp.int32) + rank))
        slot_ref[s : s + 1, :] = packed_rows[s]
    table = dot(jnp.concatenate(onehots, axis=1), jnp.concatenate(named, axis=1), NT)
    chunk = blocks * CAP + IDROWS
    sent = send_ref.reshape(owners * chunk, LANES)
    table_v[:owners, :] = table
    table_v[owners:, :] = jnp.zeros((8, LANES), F32)
    for o in range(owners):
        sent[o * chunk + blocks * CAP : (o + 1) * chunk, :] = table_v[o : o + IDROWS, :].astype(
            BF16
        )

    for copy in large:
        copy.wait()
    for s in range(subs):
        rest_v[:, s * slots_per : (s + 1) * slots_per] = dot(resid_v[s], basis_v[s]).astype(BF16)

    pick = jnp.where(
        iota((slots, slots), 0) == jnp.concatenate(packed_rows, axis=1), 1.0, 0.0
    ).astype(BF16)
    packed = dot(pick, rest_v[...], NT)
    for q in range(blocks):
        comp_v[q, :slots, :] = packed[:, q * LANES : (q + 1) * LANES]
        comp_v[q, slots:, :] = jnp.zeros((CAP, LANES), F32)

    starts = first_ref[0:1, :]
    for o in range(owners):
        rows = pl.ds(starts[0, o], CAP)
        for q in range(blocks):
            here = o * chunk + q * CAP
            sent[here : here + CAP, :] = comp_v[q, rows, :].astype(BF16)


def owner_kernel(recv_ref, inv_ref, back_ref, got_v, match_v):
    owners, _, rcols = back_ref.shape
    blocks = rcols // LANES
    cblock = inv_ref.shape[0]
    step = LANES // CAP
    chunk = blocks * CAP + IDROWS
    recv = recv_ref.reshape(owners * chunk, LANES)
    dof = iota((cblock, LANES), 0) + 1
    part_of = iota((IDROWS, LANES), 1) // CAP
    for t in range(owners // step):
        rows = slice(t * LANES, (t + 1) * LANES)
        named = jnp.zeros((IDROWS, LANES), BF16)
        for d in range(t * step, (t + 1) * step):
            ids = recv[d * chunk + blocks * CAP : (d + 1) * chunk, :]
            named = jnp.where(part_of == d % step, ids, named)
            for q in range(blocks):
                here = d * chunk + q * CAP
                got_v[d * CAP : (d + 1) * CAP, q * LANES : (q + 1) * LANES] = recv[
                    here : here + CAP, :
                ]
        named = named[0:1, :].astype(F32).astype(jnp.int32)
        match_v[:, rows] = jnp.where(dof == named, 1.0, 0.0).astype(BF16)
    total = dot(match_v[...], got_v[...])
    sol = dot(inv_ref[...], total.astype(BF16)).astype(BF16)
    part = dot(match_v[...], sol, TN).astype(BF16)
    back_ref[...] = part.reshape(owners, CAP, rcols)


def finish_kernel(
    back_ref, slot_ref, first_ref, resid_ref, inv_ref, basis_ref, out_hbm,
    comp_v, turned_v, out_v, out_sem,
):
    subs, rcols, _ = resid_ref.shape
    slots_per = basis_ref.shape[2]
    slots = subs * slots_per
    owners = back_ref.shape[0]
    blocks = rcols // LANES
    starts = first_ref[0:1, :]
    spare = comp_v.shape[1] - slots // 2
    comp_v[:, slots // 2 :, :] = jnp.zeros((blocks, spare, LANES), F32)
    for s in range(subs):
        out_v[s] = dot(resid_ref[s], inv_ref[s], NT)

    for o in range(owners):
        rows = pl.ds(starts[0, o], CAP)
        for q in range(blocks):
            comp_v[q, rows, :] = back_ref[o, :, q * LANES : (q + 1) * LANES].astype(F32)
    for q in range(blocks):
        turned_v[q * LANES : (q + 1) * LANES, :] = comp_v[q, :slots, :].astype(BF16).T
    stores = []
    for first in range(0, subs, FINISH_BATCH):
        chosen = range(first, first + FINISH_BATCH)
        packed = jnp.concatenate([slot_ref[s : s + 1, :] for s in chosen], axis=1)
        pick = jnp.where(iota((slots, packed.shape[1]), 0) == packed, 1.0, 0.0).astype(BF16)
        pulled = dot(turned_v[...], pick).astype(BF16)
        for i, s in enumerate(chosen):
            out_v[s] = out_v[s] + dot(
                pulled[:, i * slots_per : (i + 1) * slots_per], basis_ref[s], NT
            )
            copy = pltpu.make_async_copy(out_v.at[s], out_hbm.at[s], out_sem.at[s])
            copy.start()
            stores.append(copy)
    for copy in stores:
        copy.wait()


ANY = pl.BlockSpec(memory_space=pl.ANY)
HBM = pl.BlockSpec(memory_space=pltpu.HBM)
INVMEM = pl.BlockSpec(memory_space=pltpu.VMEM)


def params(mib):
    return pltpu.CompilerParams(vmem_limit_bytes=mib * 1024 * 1024)


def pack(counts, cmap, resid, basis, owners):
    subs, rcols, _ = resid.shape
    slots_per = basis.shape[2]
    shape = (owners, (rcols // LANES * CAP + IDROWS) // IDROWS, IDROWS, LANES)
    return pl.pallas_call(
        pack_kernel,
        out_shape=(
            jax.ShapeDtypeStruct(shape, BF16),
            jax.ShapeDtypeStruct((subs, slots_per), jnp.int32),
            jax.ShapeDtypeStruct((8, owners), jnp.int32),
        ),
        in_specs=[HBM, HBM, HBM, HBM],
        out_specs=(INVMEM, INVMEM, INVMEM),
        scratch_shapes=[
            pltpu.SMEM(counts.shape, jnp.int32),
            pltpu.VMEM(cmap.shape, jnp.int32),
            pltpu.VMEM(resid.shape, BF16),
            pltpu.VMEM(basis.shape, BF16),
            pltpu.VMEM((rcols, subs * slots_per), BF16),
            pltpu.VMEM((rcols // LANES, subs * slots_per + CAP, LANES), F32),
            pltpu.VMEM((owners + 8, LANES), F32),
            pltpu.SemaphoreType.DMA((2,)),
            pltpu.SemaphoreType.DMA((2,)),
        ],
        compiler_params=params(24),
        name="pack",
    )(*[pltpu.with_memory_space_constraint(x, pltpu.HBM) for x in (counts, cmap, resid, basis)])


def owner(recv, inv, rcols):
    owners = recv.shape[0]
    return pl.pallas_call(
        owner_kernel,
        out_shape=jax.ShapeDtypeStruct((owners, CAP, rcols), BF16),
        in_specs=[INVMEM, INVMEM],
        out_specs=INVMEM,
        scratch_shapes=[
            pltpu.VMEM((owners * CAP, rcols), BF16),
            pltpu.VMEM((inv.shape[0], owners * CAP), BF16),
        ],
        compiler_params=params(24),
        name="owner",
    )(recv, inv)


def finish(back, slot, first, resid, inv, basis):
    subs, rcols, _ = resid.shape
    slots = slot.size
    return pl.pallas_call(
        finish_kernel,
        out_shape=jax.ShapeDtypeStruct(resid.shape, F32),
        in_specs=[INVMEM] * 6,
        out_specs=ANY,
        scratch_shapes=[
            pltpu.VMEM((rcols // LANES, slots + CAP, LANES), F32),
            pltpu.VMEM((rcols, slots), BF16),
            pltpu.VMEM(resid.shape, F32),
            pltpu.SemaphoreType.DMA((subs,)),
        ],
        compiler_params=params(32),
        name="finish",
    )(back, slot, first, resid, inv, basis)


def per_device(resid, local_inv, basis, coarse_inv, coarse_map, row_counts):
    owners = lax.axis_size("sub") * lax.axis_size("grp")
    send, slot, first = pack(row_counts, coarse_map, resid, basis, owners)
    recv = lax.all_to_all(send, AXES, split_axis=0, concat_axis=0, tiled=True)
    back = owner(recv, coarse_inv, resid.shape[1])
    back = lax.all_to_all(back, AXES, split_axis=0, concat_axis=0, tiled=True)
    return finish(back, slot, first, resid, local_inv, basis)


def solution(mesh):
    placed = (
        P(("sub", "grp"), None, None),
        P(("sub", "grp"), None, None),
        P(("sub", "grp"), None, None),
        P(("sub", "grp"), None),
        P(("sub", "grp"), None),
        P(("sub", "grp")),
    )
    return jax.shard_map(
        per_device,
        mesh=mesh,
        in_specs=placed,
        out_specs=P(("sub", "grp"), None, None),
        check_vma=False,
    )
```
